256 devices in a mesh: rep: 8 (over z), shard: 32 (over x, y, core).
Axes of the slice: x: 4, y: 4, z: 8, core: 2. Of those that a mesh axis runs over, the one named last changes fastest.
Arguments:
- partials: bfloat16 [8, 4096, 16384], P('rep', None, 'shard'), may hold values from -45 to 45
- moment: float32 [4096, 16384], P('rep', 'shard'), may hold values from 0.5 to 50
- owner: int32 [8, 32], P('rep'), may hold values from 0 to 31, as said below
- roots: float32 [8, 32, 3, 2, 512, 512], P('rep', 'shard'), may hold values from -2 to 2, as said below
Outputs:
- direction: bfloat16 [4096, 16384], P('rep', 'shard')
- moment_new: float32 [4096, 16384], P('rep', 'shard')
The draws below stay inside these ranges and needn't reach their ends.
Inputs may be any that keep to these rules, and one draw needn't show every extreme that they name: Entry [r, c] names the owner, an index along shard, of block c of block row r. No owner holds more than 3 blocks of one row, and in every row one owner holds exactly 3. `roots`: slot k of owner o in row r holds the factors of the k-th block in column order that o owns in row r; slots past an owner's count are never read. Each matrix is symmetric.
All inputs are finite; a program needn't handle non-finite values.
Results may differ from the reference program's by a relative error of at most 0.024.
Values may be sent and summed in bfloat16 or wider, within the bound.
No kernel may reach another device: no remote copies, remote signals or barrier semaphores. Data moves between devices by JAX's collectives and lax.ppermute only.
A program may use at most 64 MiB of HBM per device.

```python
import math
import jax
import jax.numpy as jnp
from jax import lax

C = 16384
B = 512
R = 4096
MAXB = 3
N_REP = 8
N_SHARD = 32


def draw_partials(key, part):
    key = jax.random.fold_in(key, 3)
    keys = jax.random.split(key, 3)
    row_scale = jnp.exp(jax.random.uniform(keys[0], (R,), jnp.float32, math.log(0.3), math.log(3.0)))
    col_scale = jnp.exp(jax.random.uniform(keys[1], (C,), jnp.float32, math.log(0.3), math.log(3.0)))
    values = jnp.clip(jax.random.normal(keys[2], (N_REP, R, C), jnp.float32), -5.0, 5.0)
    return (values * row_scale[None, :, None] * col_scale[None, None, :]).astype(jnp.bfloat16)


def draw_owner(key, part):
    key = jax.random.fold_in(key, 7)
    block_cols = C // B

    def one_row(row_key):
        first_key, second_key, third_key = jax.random.split(row_key, 3)
        busiest = jax.random.randint(first_key, (), 0, N_SHARD, dtype=jnp.int32)
        others = (busiest + 1 + jnp.arange(N_SHARD - 1, dtype=jnp.int32)) % N_SHARD
        supply = jnp.tile(others, MAXB)
        order = jax.random.permutation(second_key, supply.shape[0])
        remaining = supply[order[:block_cols - MAXB]]
        sequence = jnp.concatenate([jnp.full((MAXB,), busiest, jnp.int32), remaining])
        placing = jax.random.permutation(third_key, block_cols)
        return sequence[placing]
    row_keys = jax.random.split(key, N_REP)
    return jax.vmap(one_row)(row_keys).astype(jnp.int32)


def draw_roots(key, part):
    key = jax.random.fold_in(key, 11)
    diag_key, noise_key = jax.random.split(key, 2)
    shape = (N_REP, N_SHARD, MAXB, 2, B, B)
    diagonal = jnp.exp(jax.random.uniform(diag_key, shape[:-1], jnp.float32, math.log(0.5), math.log(2.0)))
    noise = jnp.clip(jax.random.normal(noise_key, shape, jnp.float32), -5.0, 5.0)
    offdiag = noise * (0.4 / math.sqrt(B))
    symmetric = (offdiag + jnp.swapaxes(offdiag, -1, -2)) * 0.7071
    identity = jnp.eye(B, dtype=jnp.float32)
    return symmetric * (1.0 - identity) + identity * diagonal[..., None]


def levels(stream_key, extent, cuts, low, top_value):
    def one(axis_at, blocks):
        steps = jax.random.uniform(jax.random.fold_in(jax.random.fold_in(stream_key, 6), axis_at), (blocks,), jnp.float32, low / len(cuts), top_value / len(cuts))
        return jnp.repeat(jnp.exp(steps), extent[axis_at] // blocks).reshape((-1,) + (1,) * (len(extent) - axis_at - 1))

    gain = one(*cuts[0])
    for cut in cuts[1:]:
        gain = gain * one(*cut)
    return gain


def setup_inputs(seed: int = 0) -> dict:
    splits = jax.random.split(jax.random.key(seed), 5)
    partials = draw_partials(jax.random.fold_in(splits[4], 71), 0)
    moment = jnp.clip(jnp.exp(math.log(50.0) - 4.6051702 * jax.random.uniform(splits[1], (R, C), jnp.float32) ** levels(splits[1], (R, C), ((0, 8), (1, 32)), -0.2, 0.2)), 0.5, 50.0)
    owner = draw_owner(jax.random.fold_in(splits[4], 71), 0)
    roots = draw_roots(jax.random.fold_in(splits[4], 71), 0)
    return {"partials": partials, "moment": moment, "owner": owner, "roots": roots}


moment_decay = 0.95
adam_offset = 1e-08
norm_offset = 1e-06

def reference(partials, moment, owner, roots):
    gradient = lax.optimization_barrier(jnp.sum(partials.astype(jnp.float32), axis=0)).astype(jnp.bfloat16)
    grad_float = gradient.astype(jnp.float32)
    moment_new = moment_decay * moment + (1.0 - moment_decay) * grad_float * grad_float
    adam_step = grad_float / (jnp.sqrt(moment_new) + adam_offset)
    block_cols = C // B
    block_ids = jnp.arange(block_cols, dtype=jnp.int32)
    earlier = block_ids[None, :] < block_ids[:, None]
    same_owner = owner[:, :, None] == owner[:, None, :]
    slot_rank = lax.optimization_barrier(jnp.sum((same_owner & earlier[None]).astype(jnp.int32), axis=2))

    def one_block(block_index):
        group_id = (block_index // block_cols).astype(jnp.int32)
        column = (block_index % block_cols).astype(jnp.int32)
        row_start = (group_id * B).astype(jnp.int32)
        col_start = (column * B).astype(jnp.int32)
        grad_block = lax.dynamic_slice(grad_float, (row_start, col_start), (B, B))
        adam_block = lax.dynamic_slice(adam_step, (row_start, col_start), (B, B))
        owner_id = owner[group_id, column]
        slot_id = slot_rank[group_id, column]
        root_pair = roots[group_id, owner_id, slot_id]
        left_part = jnp.dot(root_pair[0], grad_block, precision=lax.Precision.HIGHEST, preferred_element_type=jnp.float32)
        conditioned = jnp.dot(left_part, root_pair[1], precision=lax.Precision.HIGHEST, preferred_element_type=jnp.float32)
        target = jnp.sqrt(jnp.sum(adam_block * adam_block))
        graft_scale = target / jnp.sqrt(jnp.sum(conditioned * conditioned) + norm_offset)
        return (conditioned * graft_scale).astype(jnp.bfloat16)
    blocks = lax.map(one_block, jnp.arange(N_REP * block_cols, dtype=jnp.int32))
    direction = blocks.reshape(N_REP, block_cols, B, B).transpose(0, 2, 1, 3).reshape(N_REP * B, C)
    return (direction, moment_new)
```

```python
import jax
import jax.numpy as jnp
from jax import lax
from jax.experimental import pallas as pl
from jax.experimental.pallas import tpu as pltpu
from jax.sharding import PartitionSpec as P

moment_decay = 0.95
adam_offset = 1e-08
norm_offset = 1e-06

B = 512
ROWS = 16
LANES = 128
QUARTERS = B // LANES


def iotas(shape):
    return lax.broadcasted_iota(jnp.int32, shape, 0), lax.broadcasted_iota(jnp.int32, shape, 1)


def pack_kernel(roots_ref, out_ref):
    k = pl.program_id(0)
    devices = out_ref.shape[0]
    row, col = iotas((B, LANES))
    diag_row, diag_col = iotas((LANES, LANES))
    diag_parts = []
    for q in range(QUARTERS):
        cols = slice(q * LANES, (q + 1) * LANES)
        left = roots_ref[0, 0, 0, 0, :, cols]
        right = roots_ref[0, 0, 0, 1, :, cols]
        mixed = jnp.where(row <= col + q * LANES, left, right).astype(jnp.bfloat16)
        out_ref[:, QUARTERS * k + q] = mixed.reshape(devices, ROWS, LANES)
        square = roots_ref[0, 0, 0, 1, cols, cols]
        diag_parts.append(jnp.sum(jnp.where(diag_row == diag_col, square, 0.0), axis=1, keepdims=True))
    diagonal = jnp.broadcast_to(jnp.concatenate(diag_parts, axis=0), (B, LANES))
    diagonal = diagonal.astype(jnp.bfloat16).reshape(devices, ROWS, LANES)
    lane = lax.broadcasted_iota(jnp.int32, (devices, ROWS, LANES), 2)
    last = out_ref.shape[1] - 1

    @pl.when(k == 0)
    def _():
        out_ref[:, last] = diagonal

    @pl.when(k != 0)
    def _():
        out_ref[:, last] = jnp.where(lane // 32 == k, diagonal, out_ref[:, last])


def pack(roots, devices):
    slots = roots.shape[2]
    tiles = QUARTERS * slots + 1
    return pl.pallas_call(
        pack_kernel,
        grid=(slots,),
        in_specs=[pl.BlockSpec((1, 1, 1, 2, B, B), lambda k: (0, 0, k, 0, 0, 0))],
        out_specs=pl.BlockSpec((devices, tiles, ROWS, LANES), lambda k: (0, 0, 0, 0)),
        out_shape=jax.ShapeDtypeStruct((devices, tiles, ROWS, LANES), jnp.bfloat16),
        compiler_params=pltpu.CompilerParams(vmem_limit_bytes=24 * 1024 * 1024),
        cost_estimate=pl.CostEstimate(flops=0, bytes_accessed=8 * 1024 * 1024, transcendentals=0),
    )(roots)


def pick_kernel(owner_ref, slot_ref, in_ref, out_ref):
    last = in_ref.shape[1] - 1

    def one(c, carry):
        o = owner_ref[c]
        s = slot_ref[c]
        for q in range(QUARTERS):
            out_ref[c, q] = in_ref[o, QUARTERS * s + q]
        out_ref[c, QUARTERS] = in_ref[o, last]
        return carry

    lax.fori_loop(0, out_ref.shape[0], one, 0)


def pick(owner_row, slot_rank, pieces):
    cols = owner_row.shape[0]
    return pl.pallas_call(
        pick_kernel,
        in_specs=[
            pl.BlockSpec(memory_space=pltpu.SMEM),
            pl.BlockSpec(memory_space=pltpu.SMEM),
            pl.BlockSpec(memory_space=pltpu.VMEM),
        ],
        out_specs=pl.BlockSpec(memory_space=pltpu.VMEM),
        out_shape=jax.ShapeDtypeStruct((cols, QUARTERS + 1, ROWS, LANES), jnp.bfloat16),
        compiler_params=pltpu.CompilerParams(vmem_limit_bytes=16 * 1024 * 1024),
        cost_estimate=pl.CostEstimate(flops=0, bytes_accessed=3 * 1024 * 1024, transcendentals=0),
    )(owner_row, slot_rank, pieces)


def unpack_kernel(slot_ref, in_ref, left_ref, right_ref):
    slot = slot_ref[0]
    row, col = iotas((LANES, LANES))
    for i in range(QUARTERS):
        rows = slice(i * LANES, (i + 1) * LANES)
        chunk = LANES // ROWS
        members = slice(i * chunk, (i + 1) * chunk)
        tile = in_ref[members, QUARTERS].reshape(LANES, LANES).astype(jnp.float32)
        diagonal = jnp.sum(jnp.where(col == slot * 32, tile, 0.0), axis=1, keepdims=True)
        for j in range(i, QUARTERS):
            cols = slice(j * LANES, (j + 1) * LANES)
            upper = in_ref[members, j].reshape(LANES, LANES).astype(jnp.float32)
            if i == j:
                turned = upper.T
                left_ref[rows, cols] = jnp.where(row <= col, upper, turned).astype(jnp.bfloat16)
                right = jnp.where(row > col, upper, turned)
                right_ref[rows, cols] = jnp.where(row == col, diagonal, right).astype(jnp.bfloat16)
            else:
                others = slice(j * chunk, (j + 1) * chunk)
                lower = in_ref[others, i].reshape(LANES, LANES).astype(jnp.float32)
                left_ref[rows, cols] = upper.astype(jnp.bfloat16)
                left_ref[cols, rows] = upper.T.astype(jnp.bfloat16)
                right_ref[cols, rows] = lower.astype(jnp.bfloat16)
                right_ref[rows, cols] = lower.T.astype(jnp.bfloat16)


def unpack(slot, pieces):
    whole = jax.ShapeDtypeStruct((B, B), jnp.bfloat16)
    return pl.pallas_call(
        unpack_kernel,
        in_specs=[pl.BlockSpec(memory_space=pltpu.SMEM), pl.BlockSpec(memory_space=pltpu.VMEM)],
        out_specs=[pl.BlockSpec(memory_space=pltpu.VMEM)] * 2,
        out_shape=[whole, whole],
        compiler_params=pltpu.CompilerParams(vmem_limit_bytes=16 * 1024 * 1024),
        cost_estimate=pl.CostEstimate(flops=0, bytes_accessed=2 * 1024 * 1024, transcendentals=0),
    )(slot, pieces)


def finish_kernel(grad_ref, moment_ref, left_ref, right_ref, direction_ref, moment_out_ref):
    gradient = grad_ref[...]
    grad_float = gradient.astype(jnp.float32)
    moment_new = moment_decay * moment_ref[...] + (1.0 - moment_decay) * grad_float * grad_float
    moment_out_ref[...] = moment_new
    adam_step = grad_float / (jnp.sqrt(moment_new) + adam_offset)
    target = jnp.sqrt(jnp.sum(adam_step * adam_step))
    left_part = jnp.dot(left_ref[...], gradient, preferred_element_type=jnp.float32)
    conditioned = jnp.dot(
        left_part.astype(jnp.bfloat16), right_ref[...], preferred_element_type=jnp.float32
    )
    scale = target / jnp.sqrt(jnp.sum(conditioned * conditioned) + norm_offset)
    direction_ref[...] = (conditioned * scale).astype(jnp.bfloat16)


def finish(gradient, moment, left, right):
    return pl.pallas_call(
        finish_kernel,
        in_specs=[pl.BlockSpec(memory_space=pltpu.VMEM)] * 4,
        out_specs=[pl.BlockSpec(memory_space=pltpu.VMEM)] * 2,
        out_shape=[
            jax.ShapeDtypeStruct((B, B), jnp.bfloat16),
            jax.ShapeDtypeStruct((B, B), jnp.float32),
        ],
        compiler_params=pltpu.CompilerParams(vmem_limit_bytes=32 * 1024 * 1024),
        cost_estimate=pl.CostEstimate(
            flops=4 * B * B * B, bytes_accessed=5 * 1024 * 1024, transcendentals=0
        ),
    )(gradient, moment, left, right)


def body(partials, moment, owner, roots):
    devices = lax.axis_size("shard")
    gradient = lax.psum_scatter(partials, "rep", scatter_dimension=1, tiled=True)[0]
    owner_row = owner[0]
    block_ids = jnp.arange(owner_row.shape[0], dtype=jnp.int32)
    earlier = block_ids[None, :] < block_ids[:, None]
    same_owner = owner_row[:, None] == owner_row[None, :]
    slot_rank = jnp.sum((same_owner & earlier).astype(jnp.int32), axis=1)
    own_slot = lax.dynamic_slice_in_dim(slot_rank, lax.axis_index("shard"), 1)
    packed = pack(roots, devices)
    pieces = lax.all_to_all(packed, "shard", split_axis=0, concat_axis=0, tiled=True)
    picked = pick(owner_row, slot_rank, pieces)
    arrived = lax.all_to_all(picked, "shard", split_axis=0, concat_axis=0, tiled=True)
    left, right = unpack(own_slot, arrived)
    return tuple(finish(gradient, moment, left, right))


def solution(mesh):
    placed = (
        P("rep", None, "shard"),
        P("rep", "shard"),
        P("rep", None),
        P("rep", "shard", None, None, None, None),
    )
    return jax.shard_map(
        body,
        mesh=mesh,
        in_specs=placed,
        out_specs=(P("rep", "shard"), P("rep", "shard")),
        check_vma=False,
    )
```

```python
import jax
import jax.numpy as jnp
from jax import lax
from jax.experimental import pallas as pl
from jax.experimental.pallas import tpu as pltpu
from jax.sharding import PartitionSpec as P

moment_decay = 0.95
adam_offset = 1e-08
norm_offset = 1e-06

B = 512
ROWS = 16
FULL = 60 * 1024 * 1024
LANES = 128
QUARTERS = B // LANES


def iotas(shape):
    return lax.broadcasted_iota(jnp.int32, shape, 0), lax.broadcasted_iota(jnp.int32, shape, 1)


def pack_kernel(roots_ref, out_ref, held, sems):
    slots = roots_ref.shape[2]
    devices, tiles = out_ref.shape[:2]
    rows = B // PARTS
    members = devices // PARTS
    copies = []
    for k in range(slots):
        for p in range(PARTS):
            copies.append(
                pltpu.make_async_copy(
                    roots_ref.at[0, 0, k, :, p * rows : (p + 1) * rows, :],
                    held.at[k, :, p * rows : (p + 1) * rows, :],
                    sems.at[k, p],
                )
            )
    for copy in copies:
        copy.start()
    row, col = iotas((rows, LANES))
    diag_row, diag_col = iotas((LANES, LANES))
    lane = lax.broadcasted_iota(jnp.int32, (rows, LANES), 1)
    diagonal = [jnp.zeros((rows, LANES), jnp.float32)] * PARTS
    for k in range(slots):
        for p in range(PARTS):
            copies[k * PARTS + p].wait()
            here = slice(p * rows, (p + 1) * rows)
            group = slice(p * members, (p + 1) * members)
            parts = []
            for q in range(QUARTERS):
                cols = slice(q * LANES, (q + 1) * LANES)
                left = held[k, 0, here, cols]
                right = held[k, 1, here, cols]
                mixed = jnp.where(row + p * rows <= col + q * LANES, left, right)
                out_ref[group, QUARTERS * k + q] = mixed.astype(jnp.bfloat16).reshape(
                    members, ROWS, LANES
                )
                if p * rows <= q * LANES < (p + 1) * rows:
                    square = held[k, 1, q * LANES : (q + 1) * LANES, cols]
                    parts.append(
                        jnp.sum(jnp.where(diag_row == diag_col, square, 0.0), axis=1, keepdims=True)
                    )
            spread = jnp.broadcast_to(jnp.concatenate(parts, axis=0), (rows, LANES))
            diagonal[p] = jnp.where(lane // 32 == k, spread, diagonal[p])
    for p in range(PARTS):
        out_ref[p * members : (p + 1) * members, tiles - 1] = (
            diagonal[p].astype(jnp.bfloat16).reshape(members, ROWS, LANES)
        )


PARTS = 2
PACKCOST = 0


def pack(roots, devices):
    slots = roots.shape[2]
    tiles = QUARTERS * slots + 1
    return pl.pallas_call(
        pack_kernel,
        in_specs=[pl.BlockSpec(memory_space=pl.ANY)],
        out_specs=pl.BlockSpec(memory_space=pltpu.VMEM),
        out_shape=jax.ShapeDtypeStruct((devices, tiles, ROWS, LANES), jnp.bfloat16),
        scratch_shapes=[
            pltpu.VMEM((slots, 2, B, B), jnp.float32),
            pltpu.SemaphoreType.DMA((slots, PARTS)),
        ],
        compiler_params=pltpu.CompilerParams(vmem_limit_bytes=58 * 1024 * 1024),
        cost_estimate=pl.CostEstimate(flops=PACKCOST, bytes_accessed=8 * 1024 * 1024, transcendentals=0),
        name="pack",
    )(roots)


def pick_kernel(owner_ref, in_ref, out_ref, counts):
    devices, tiles = in_ref.shape[:2]
    lane = lax.broadcasted_iota(jnp.int32, (ROWS, LANES), 1)
    for o in range(devices):
        counts[o] = 0
    for c in range(out_ref.shape[0]):
        o = owner_ref[0, c]
        slot = counts[o]
        counts[o] = slot + 1
        for q in range(QUARTERS):
            out_ref[c, q] = in_ref[o, QUARTERS * slot + q]
        diagonal = in_ref[o, tiles - 1].astype(jnp.float32)
        kept = jnp.where(lane == slot * 32, diagonal, 0.0)
        out_ref[c, QUARTERS] = kept.astype(jnp.bfloat16)


def pick(owner, pieces):
    cols = owner.shape[1]
    return pl.pallas_call(
        pick_kernel,
        in_specs=[pl.BlockSpec(memory_space=pltpu.SMEM), pl.BlockSpec(memory_space=pltpu.VMEM)],
        out_specs=pl.BlockSpec(memory_space=pltpu.VMEM),
        out_shape=jax.ShapeDtypeStruct((cols, QUARTERS + 1, ROWS, LANES), jnp.bfloat16),
        scratch_shapes=[pltpu.SMEM((pieces.shape[0],), jnp.int32)],
        compiler_params=pltpu.CompilerParams(vmem_limit_bytes=8 * 1024 * 1024),
        cost_estimate=pl.CostEstimate(flops=0, bytes_accessed=3 * 1024 * 1024, transcendentals=0),
        name="pick",
    )(owner, pieces)


def unpack_kernel(in_ref, left_ref, right_ref):
    row, col = iotas((LANES, LANES))
    for i in range(QUARTERS):
        rows = slice(i * LANES, (i + 1) * LANES)
        chunk = LANES // ROWS
        members = slice(i * chunk, (i + 1) * chunk)
        tile = in_ref[members, QUARTERS].reshape(LANES, LANES).astype(jnp.float32)
        diagonal = jnp.sum(tile, axis=1, keepdims=True)
        for j in range(i, QUARTERS):
            cols = slice(j * LANES, (j + 1) * LANES)
            upper = in_ref[members, j].reshape(LANES, LANES).astype(jnp.float32)
            if i == j:
                turned = upper.T
                left_ref[rows, cols] = jnp.where(row <= col, upper, turned).astype(jnp.bfloat16)
                right = jnp.where(row > col, upper, turned)
                right_ref[rows, cols] = jnp.where(row == col, diagonal, right).astype(jnp.bfloat16)
            else:
                others = slice(j * chunk, (j + 1) * chunk)
                lower = in_ref[others, i].reshape(LANES, LANES).astype(jnp.float32)
                left_ref[rows, cols] = upper.astype(jnp.bfloat16)
                left_ref[cols, rows] = upper.T.astype(jnp.bfloat16)
                right_ref[cols, rows] = lower.astype(jnp.bfloat16)
                right_ref[rows, cols] = lower.T.astype(jnp.bfloat16)


def unpack(pieces):
    whole = jax.ShapeDtypeStruct((B, B), jnp.bfloat16)
    return pl.pallas_call(
        unpack_kernel,
        in_specs=[pl.BlockSpec(memory_space=pltpu.VMEM)],
        out_specs=[pl.BlockSpec(memory_space=pltpu.VMEM)] * 2,
        out_shape=[whole, whole],
        compiler_params=pltpu.CompilerParams(vmem_limit_bytes=8 * 1024 * 1024),
        cost_estimate=pl.CostEstimate(flops=0, bytes_accessed=2 * 1024 * 1024, transcendentals=0),
        name="unpack",
    )(pieces)


def finish_kernel(
    own_ref, up_ref, down_ref, up_last_ref, down_last_ref, moment_ref, left_ref, right_ref,
    direction_ref, moment_out_ref,
):
    own = own_ref[...].astype(jnp.float32)
    up = jnp.concatenate([up_last_ref[...], up_ref[HALF:]], axis=0).astype(jnp.float32)
    down = jnp.concatenate([down_ref[:HALF], down_last_ref[...]], axis=0).astype(jnp.float32)
    gradient = (own + up + down).astype(jnp.bfloat16)
    grad_float = gradient.astype(jnp.float32)
    moment_new = moment_decay * moment_ref[...] + (1.0 - moment_decay) * grad_float * grad_float
    moment_out_ref[...] = moment_new
    adam_step = grad_float / (jnp.sqrt(moment_new) + adam_offset)
    target = jnp.sqrt(jnp.sum(adam_step * adam_step))
    left_part = jnp.dot(left_ref[...], gradient, preferred_element_type=jnp.float32)
    conditioned = jnp.dot(
        left_part.astype(jnp.bfloat16), right_ref[...], preferred_element_type=jnp.float32
    )
    scale = target / jnp.sqrt(jnp.sum(conditioned * conditioned) + norm_offset)
    direction_ref[...] = (conditioned * scale).astype(jnp.bfloat16)


def finish(sums, moment, left, right):
    return pl.pallas_call(
        finish_kernel,
        in_specs=[pl.BlockSpec(memory_space=pltpu.VMEM)] * 8,
        out_specs=[pl.BlockSpec(memory_space=pltpu.VMEM)] * 2,
        out_shape=[
            jax.ShapeDtypeStruct((B, B), jnp.bfloat16),
            jax.ShapeDtypeStruct((B, B), jnp.float32),
        ],
        compiler_params=pltpu.CompilerParams(vmem_limit_bytes=24 * 1024 * 1024),
        cost_estimate=pl.CostEstimate(
            flops=4 * B * B * B, bytes_accessed=5 * 1024 * 1024, transcendentals=0
        ),
    )(*sums, moment, left, right)


HALF = B // 2


def reduce_chunks(partials, packed):
    groups = lax.axis_size("rep")
    pairs_up = [(k, (k + 1) % groups) for k in range(groups)]
    pairs_down = [(k, (k - 1) % groups) for k in range(groups)]

    def move(up, down):
        return lax.ppermute(up, "rep", pairs_up), lax.ppermute(down, "rep", pairs_down)

    def mine(offset, start=0, rows=B):
        chunk = lax.rem(lax.axis_index("rep") + offset + groups, groups)
        return lax.dynamic_slice(partials, (chunk * B + start, 0), (rows, B))

    def add(a, b):
        return (a.astype(jnp.float32) + b.astype(jnp.float32)).astype(jnp.bfloat16)

    def pair(first, second):
        return mine(first, 0, HALF), mine(second, HALF, HALF)

    def join(arrived, parts):
        return jnp.concatenate([add(arrived[:HALF], parts[0]), add(arrived[HALF:], parts[1])])

    up, down = move(jnp.concatenate(pair(4, 3)), jnp.concatenate(pair(-3, -4)))
    up, down, packed = lax.optimization_barrier((up, down, packed))
    up, down = move(*lax.optimization_barrier((join(up, pair(3, 2)), join(down, pair(-2, -3)))))
    up, down = lax.optimization_barrier((up, down))
    up, down = move(*lax.optimization_barrier((join(up, pair(2, 1)), join(down, pair(-1, -2)))))
    up, down = lax.optimization_barrier((up, down))
    up_last, down_last = move(
        *lax.optimization_barrier(
            (add(up[:HALF], mine(1, 0, HALF)), add(down[HALF:], mine(-1, HALF, HALF)))
        )
    )
    return (mine(0), up, down, up_last, down_last), packed


def body(partials, moment, owner, roots):
    devices = lax.axis_size("shard")
    packed = pack(roots, devices)
    sums, _ = reduce_chunks(partials[0], packed)
    pieces = lax.all_to_all(packed, "shard", split_axis=0, concat_axis=0, tiled=True)
    picked = pick(owner, pieces)
    arrived = lax.all_to_all(picked, "shard", split_axis=0, concat_axis=0, tiled=True)
    left, right = unpack(arrived)
    return tuple(finish(sums, moment, left, right))


def solution(mesh):
    placed = (
        P("rep", None, "shard"),
        P("rep", "shard"),
        P("rep", None),
        P("rep", "shard", None, None, None, None),
    )
    return jax.shard_map(
        body,
        mesh=mesh,
        in_specs=placed,
        out_specs=(P("rep", "shard"), P("rep", "shard")),
        check_vma=False,
    )
```

```python
import jax
import jax.numpy as jnp
from jax import lax
from jax.experimental import pallas as pl
from jax.experimental.pallas import tpu as pltpu
from jax.sharding import PartitionSpec as P

moment_decay = 0.95
adam_offset = 1e-08
norm_offset = 1e-06

B = 512
ROWS = 16
FULL = 60 * 1024 * 1024
LANES = 128
QUARTERS = B // LANES


def iotas(shape):
    return lax.broadcasted_iota(jnp.int32, shape, 0), lax.broadcasted_iota(jnp.int32, shape, 1)


def pack_kernel(roots_ref, out_ref, held, sems):
    slots = roots_ref.shape[2]
    tiles = out_ref.shape[1]
    chunk = LANES // ROWS
    copies = {}
    for k in range(slots):
        for i in range(QUARTERS):
            rows = slice(i * LANES, (i + 1) * LANES)
            for side, cols in ((0, slice(i * LANES, B)), (1, slice(0, (i + 1) * LANES))):
                copies[k, i, side] = pltpu.make_async_copy(
                    roots_ref.at[0, 0, k, side, rows, cols],
                    held.at[k, side, rows, cols],
                    sems.at[k, i, side],
                )
                copies[k, i, side].start()
    row, col = iotas((LANES, LANES))
    diagonal = [jnp.zeros((LANES, LANES), jnp.float32)] * QUARTERS
    for k in range(slots):
        for i in range(QUARTERS):
            rows = slice(i * LANES, (i + 1) * LANES)
            copies[k, i, 0].wait()
            copies[k, i, 1].wait()
            for j in range(QUARTERS):
                cols = slice(j * LANES, (j + 1) * LANES)
                if i == j:
                    right = held[k, 1, rows, cols]
                    block = jnp.where(row <= col, held[k, 0, rows, cols], right)
                    only = jnp.sum(jnp.where(row == col, right, 0.0), axis=1, keepdims=True)
                    diagonal[i] = jnp.where(col // 32 == k, only, diagonal[i])
                else:
                    block = held[k, 0 if i < j else 1, rows, cols]
                out_ref[i * chunk : (i + 1) * chunk, QUARTERS * k + j] = block.astype(
                    jnp.bfloat16
                ).reshape(chunk, ROWS, LANES)
    for i in range(QUARTERS):
        out_ref[i * chunk : (i + 1) * chunk, tiles - 1] = (
            diagonal[i].astype(jnp.bfloat16).reshape(chunk, ROWS, LANES)
        )


def pack(roots, devices):
    slots = roots.shape[2]
    tiles = QUARTERS * slots + 1
    return pl.pallas_call(
        pack_kernel,
        in_specs=[pl.BlockSpec(memory_space=pl.ANY)],
        out_specs=pl.BlockSpec(memory_space=pltpu.VMEM),
        out_shape=jax.ShapeDtypeStruct((devices, tiles, ROWS, LANES), jnp.bfloat16),
        scratch_shapes=[
            pltpu.VMEM((slots, 2, B, B), jnp.float32),
            pltpu.SemaphoreType.DMA((slots, QUARTERS, 2)),
        ],
        compiler_params=pltpu.CompilerParams(vmem_limit_bytes=58 * 1024 * 1024),
        cost_estimate=pl.CostEstimate(flops=0, bytes_accessed=8 * 1024 * 1024, transcendentals=0),
        name="pack",
    )(roots)


def pick_kernel(owner_ref, in_ref, out_ref, counts):
    devices, tiles = in_ref.shape[:2]
    lane = lax.broadcasted_iota(jnp.int32, (ROWS, LANES), 1)
    for o in range(devices):
        counts[o] = 0
    owners = owner_ref[...]
    for c in range(out_ref.shape[0]):
        o = owners[0, c]
        slot = counts[o]
        counts[o] = slot + 1
        for q in range(QUARTERS):
            out_ref[c, q] = in_ref[o, QUARTERS * slot + q]
        diagonal = in_ref[o, tiles - 1].astype(jnp.float32)
        kept = jnp.where(lane == slot * 32, diagonal, 0.0)
        out_ref[c, QUARTERS] = kept.astype(jnp.bfloat16)


def pick(owner, pieces):
    cols = owner.shape[1]
    return pl.pallas_call(
        pick_kernel,
        in_specs=[pl.BlockSpec(memory_space=pltpu.VMEM)] * 2,
        out_specs=pl.BlockSpec(memory_space=pltpu.VMEM),
        out_shape=jax.ShapeDtypeStruct((cols, QUARTERS + 1, ROWS, LANES), jnp.bfloat16),
        scratch_shapes=[pltpu.SMEM((pieces.shape[0],), jnp.int32)],
        compiler_params=pltpu.CompilerParams(vmem_limit_bytes=8 * 1024 * 1024),
        cost_estimate=pl.CostEstimate(flops=0, bytes_accessed=3 * 1024 * 1024, transcendentals=0),
        name="pick",
    )(owner, pieces)


def adam_kernel(
    own_ref, up_a_ref, up_b_ref, down_a_ref, down_b_ref, moment_ref,
    gradient_ref, moment_out_ref, target_ref,
):
    total = jnp.float32(0.0)
    first, second = slice(0, HALF), slice(HALF, B)
    for rows, up, down in (
        (first, up_a_ref[...], down_a_ref[...]),
        (second, up_b_ref[...], down_b_ref[...]),
    ):
        own = own_ref[rows].astype(jnp.float32)
        summed = own + up.astype(jnp.float32) + down.astype(jnp.float32)
        gradient = summed.astype(jnp.bfloat16)
        gradient_ref[rows] = gradient
        grad_float = gradient.astype(jnp.float32)
        moment_new = (
            moment_decay * moment_ref[rows] + (1.0 - moment_decay) * grad_float * grad_float
        )
        moment_out_ref[rows] = moment_new
        adam_step = grad_float / (jnp.sqrt(moment_new) + adam_offset)
        total += jnp.sum(adam_step * adam_step)
    target_ref[...] = jnp.broadcast_to(jnp.sqrt(total), target_ref.shape)


def adam(sums, moment):
    return pl.pallas_call(
        adam_kernel,
        in_specs=[pl.BlockSpec(memory_space=pltpu.VMEM)] * 6,
        out_specs=[pl.BlockSpec(memory_space=pltpu.VMEM)] * 3,
        out_shape=[
            jax.ShapeDtypeStruct((B, B), jnp.bfloat16),
            jax.ShapeDtypeStruct((B, B), jnp.float32),
            jax.ShapeDtypeStruct((1, LANES), jnp.float32),
        ],
        compiler_params=pltpu.CompilerParams(vmem_limit_bytes=16 * 1024 * 1024),
        cost_estimate=pl.CostEstimate(flops=0, bytes_accessed=5 * 1024 * 1024, transcendentals=0),
        name="adam",
    )(*sums, moment)


def direction_kernel(in_ref, gradient_ref, target_ref, direction_ref, left_ref, right_ref):
    row, col = iotas((LANES, LANES))
    chunk = LANES // ROWS
    for i in range(QUARTERS):
        rows = slice(i * LANES, (i + 1) * LANES)
        members = slice(i * chunk, (i + 1) * chunk)
        tile = in_ref[members, QUARTERS].reshape(LANES, LANES).astype(jnp.float32)
        diagonal = jnp.sum(tile, axis=1, keepdims=True)
        for j in range(i, QUARTERS):
            cols = slice(j * LANES, (j + 1) * LANES)
            upper = in_ref[members, j].reshape(LANES, LANES).astype(jnp.float32)
            if i == j:
                turned = upper.T
                left_ref[rows, cols] = jnp.where(row <= col, upper, turned).astype(jnp.bfloat16)
                right = jnp.where(row > col, upper, turned)
                right_ref[rows, cols] = jnp.where(row == col, diagonal, right).astype(jnp.bfloat16)
            else:
                others = slice(j * chunk, (j + 1) * chunk)
                lower = in_ref[others, i].reshape(LANES, LANES).astype(jnp.float32)
                left_ref[rows, cols] = upper.astype(jnp.bfloat16)
                left_ref[cols, rows] = upper.T.astype(jnp.bfloat16)
                right_ref[cols, rows] = lower.astype(jnp.bfloat16)
                right_ref[rows, cols] = lower.T.astype(jnp.bfloat16)
    left_part = jnp.dot(left_ref[...], gradient_ref[...], preferred_element_type=jnp.float32)
    conditioned = jnp.dot(
        left_part.astype(jnp.bfloat16), right_ref[...], preferred_element_type=jnp.float32
    )
    scale = target_ref[:, :1] / jnp.sqrt(jnp.sum(conditioned * conditioned) + norm_offset)
    direction_ref[...] = (conditioned * scale).astype(jnp.bfloat16)


def direct(pieces, gradient, target):
    return pl.pallas_call(
        direction_kernel,
        in_specs=[pl.BlockSpec(memory_space=pltpu.VMEM)] * 3,
        out_specs=pl.BlockSpec(memory_space=pltpu.VMEM),
        out_shape=jax.ShapeDtypeStruct((B, B), jnp.bfloat16),
        scratch_shapes=[pltpu.VMEM((B, B), jnp.bfloat16)] * 2,
        compiler_params=pltpu.CompilerParams(vmem_limit_bytes=16 * 1024 * 1024),
        cost_estimate=pl.CostEstimate(
            flops=4 * B * B * B, bytes_accessed=2 * 1024 * 1024, transcendentals=0
        ),
        name="direction",
    )(pieces, gradient, target)


HALF = B // 2


def add_kernel(up_ref, down_ref, up_own_ref, down_own_ref, up_out_ref, down_out_ref):
    for in_ref, own_ref, out_ref in (
        (up_ref, up_own_ref, up_out_ref),
        (down_ref, down_own_ref, down_out_ref),
    ):
        total = in_ref[...].astype(jnp.float32) + own_ref[...].astype(jnp.float32)
        out_ref[...] = total.astype(jnp.bfloat16)


def add_own(up, down, own, name, flops=40*10**8):
    return pl.pallas_call(
        add_kernel,
        in_specs=[pl.BlockSpec(memory_space=pltpu.VMEM)] * (2 + len(own)),
        out_specs=[pl.BlockSpec(memory_space=pltpu.VMEM)] * 2,
        out_shape=[jax.ShapeDtypeStruct((HALF, B), jnp.bfloat16)] * 2,
        compiler_params=pltpu.CompilerParams(vmem_limit_bytes=8 * 1024 * 1024),
        cost_estimate=pl.CostEstimate(flops=flops, bytes_accessed=3 * 1024 * 1024, transcendentals=0),
        name=name,
    )(up, down, *own)


def reduce_chunks(partials, packed):
    groups = lax.axis_size("rep")
    pairs_up = [(k, (k + 1) % groups) for k in range(groups)]
    pairs_down = [(k, (k - 1) % groups) for k in range(groups)]

    def move(up, down):
        return lax.ppermute(up, "rep", pairs_up), lax.ppermute(down, "rep", pairs_down)

    def mine(offset, start=0, rows=B, source=partials):
        chunk = lax.rem(lax.axis_index("rep") + offset + groups, groups)
        return lax.dynamic_slice(source, (chunk * B + start, 0), (rows, B))

    def add(a, b):
        return (a.astype(jnp.float32) + b.astype(jnp.float32)).astype(jnp.bfloat16)

    def half(offset, part, source=partials):
        return mine(offset, part * HALF, HALF, source)

    def parts(step, part, source=partials):
        return [half(step, part, source), half(-step, 1 - part, source)]

    barrier = lax.optimization_barrier
    up, down = move(
        jnp.concatenate([half(4, 0), half(3, 1)]), jnp.concatenate([half(-3, 0), half(-4, 1)])
    )
    up, down, packed = barrier((up, down, packed))
    own = parts(3, 0)
    sent = barrier((add(up[:HALF], own[0]), add(down[HALF:], own[1])))
    long = move(*sent)
    up, down, later, _ = barrier((up, down, partials, sent))
    own = parts(2, 1, later)
    sent = barrier((add(up[HALF:], own[0]), add(down[:HALF], own[1])))
    short = move(*sent)
    later, _ = barrier((later, sent))
    long = move(*add_own(*long, parts(2, 0, later), "long_3"))
    sent = add_own(*short, parts(1, 1, later), "short_3")
    short = move(*sent)
    later, _ = barrier((later, sent))
    long = move(*add_own(*long, parts(1, 0, later), "long_4"))
    return mine(0, source=later), long[0], short[0], short[1], long[1]


def body(partials, moment, owner, roots):
    devices = lax.axis_size("shard")
    packed = pack(roots, devices)
    sums = reduce_chunks(partials[0], packed)
    pieces = lax.all_to_all(packed, "shard", split_axis=0, concat_axis=0, tiled=True)
    picked = pick(owner, pieces)
    arrived = lax.all_to_all(picked, "shard", split_axis=0, concat_axis=0, tiled=True)
    gradient, moment_new, target = adam(sums, moment)
    return direct(arrived, gradient, target), moment_new


def solution(mesh):
    placed = (
        P("rep", None, "shard"),
        P("rep", "shard"),
        P("rep", None),
        P("rep", "shard", None, None, None, None),
    )
    return jax.shard_map(
        body,
        mesh=mesh,
        in_specs=placed,
        out_specs=(P("rep", "shard"), P("rep", "shard")),
        check_vma=False,
    )
```

```python
import jax
import jax.numpy as jnp
from jax import lax
from jax.experimental import pallas as pl
from jax.experimental.pallas import tpu as pltpu
from jax.sharding import PartitionSpec as P

moment_decay = 0.95
adam_offset = 1e-08
norm_offset = 1e-06

B = 512
ROWS = 16
FULL = 60 * 1024 * 1024
LANES = 128
QUARTERS = B // LANES


def iotas(shape):
    return lax.broadcasted_iota(jnp.int32, shape, 0), lax.broadcasted_iota(jnp.int32, shape, 1)


def pack_kernel(roots_ref, result_ref, held, out_ref, sems, out_sems):
    slots = roots_ref.shape[2]
    tiles = result_ref.shape[1]
    chunk = LANES // ROWS
    copies = {}
    for k in range(slots):
        for i in range(QUARTERS):
            rows = slice(i * LANES, (i + 1) * LANES)
            for side, cols in ((0, slice(i * LANES, B)), (1, slice(0, (i + 1) * LANES))):
                copies[k, i, side] = pltpu.make_async_copy(
                    roots_ref.at[0, 0, k, side, rows, cols],
                    held.at[k, side, rows, cols],
                    sems.at[k, i, side],
                )
                copies[k, i, side].start()
    row, col = iotas((LANES, LANES))
    diagonal = [jnp.zeros((LANES, LANES), jnp.float32)] * QUARTERS
    stores = []
    for k in range(slots):
        for i in range(QUARTERS):
            rows = slice(i * LANES, (i + 1) * LANES)
            copies[k, i, 0].wait()
            copies[k, i, 1].wait()
            for j in range(QUARTERS):
                cols = slice(j * LANES, (j + 1) * LANES)
                if i == j:
                    right = held[k, 1, rows, cols]
                    block = jnp.where(row <= col, held[k, 0, rows, cols], right)
                    only = jnp.sum(jnp.where(row == col, right, 0.0), axis=1, keepdims=True)
                    diagonal[i] = jnp.where(col // 32 == k, only, diagonal[i])
                else:
                    block = held[k, 0 if i < j else 1, rows, cols]
                out_ref[i * chunk : (i + 1) * chunk, QUARTERS * k + j] = block.astype(
                    jnp.bfloat16
                ).reshape(chunk, ROWS, LANES)
            members = slice(i * chunk, (i + 1) * chunk)
            ready = slice(QUARTERS * k, QUARTERS * (k + 1))
            if k == slots - 1:
                out_ref[members, tiles - 1] = (
                    diagonal[i].astype(jnp.bfloat16).reshape(chunk, ROWS, LANES)
                )
                ready = slice(QUARTERS * k, tiles)
            stores.append(
                pltpu.make_async_copy(
                    out_ref.at[members, ready], result_ref.at[members, ready], out_sems.at[k, i]
                )
            )
            stores[-1].start()
    for store in stores:
        store.wait()


def pack(roots, devices):
    slots = roots.shape[2]
    tiles = QUARTERS * slots + 1
    return pl.pallas_call(
        pack_kernel,
        in_specs=[pl.BlockSpec(memory_space=pl.ANY)],
        out_specs=pl.BlockSpec(memory_space=pl.ANY),
        out_shape=jax.ShapeDtypeStruct((devices, tiles, ROWS, LANES), jnp.bfloat16),
        scratch_shapes=[
            pltpu.VMEM((slots, 2, B, B), jnp.float32),
            pltpu.VMEM((devices, tiles, ROWS, LANES), jnp.bfloat16),
            pltpu.SemaphoreType.DMA((slots, QUARTERS, 2)),
            pltpu.SemaphoreType.DMA((slots, QUARTERS)),
        ],
        compiler_params=pltpu.CompilerParams(vmem_limit_bytes=58 * 1024 * 1024),
        cost_estimate=pl.CostEstimate(flops=0, bytes_accessed=8 * 1024 * 1024, transcendentals=0),
        name="pack",
    )(roots)


def pick_kernel(owner_ref, in_ref, out_ref, counts):
    devices, tiles = in_ref.shape[:2]
    lane = lax.broadcasted_iota(jnp.int32, (ROWS, LANES), 1)
    for o in range(devices):
        counts[o] = 0
    owners = owner_ref[...]
    for c in range(out_ref.shape[0]):
        o = owners[0, c]
        slot = counts[o]
        counts[o] = slot + 1
        for q in range(QUARTERS):
            out_ref[c, q] = in_ref[o, QUARTERS * slot + q]
        diagonal = in_ref[o, tiles - 1].astype(jnp.float32)
        kept = jnp.where(lane == slot * 32, diagonal, 0.0)
        out_ref[c, QUARTERS] = kept.astype(jnp.bfloat16)


def pick(owner, pieces):
    cols = owner.shape[1]
    return pl.pallas_call(
        pick_kernel,
        in_specs=[pl.BlockSpec(memory_space=pltpu.VMEM)] * 2,
        out_specs=pl.BlockSpec(memory_space=pltpu.VMEM),
        out_shape=jax.ShapeDtypeStruct((cols, QUARTERS + 1, ROWS, LANES), jnp.bfloat16),
        scratch_shapes=[pltpu.SMEM((pieces.shape[0],), jnp.int32)],
        compiler_params=pltpu.CompilerParams(vmem_limit_bytes=8 * 1024 * 1024),
        cost_estimate=pl.CostEstimate(flops=0, bytes_accessed=3 * 1024 * 1024, transcendentals=0),
        name="pick",
    )(owner, pieces)


def adam_kernel(
    own_ref, up_a_ref, up_b_ref, down_a_ref, down_b_ref, moment_ref,
    gradient_ref, moment_out_ref, target_ref,
):
    total = jnp.float32(0.0)
    first, second = slice(0, HALF), slice(HALF, B)
    for rows, up, down in (
        (first, up_a_ref[...], down_a_ref[...]),
        (second, up_b_ref[...], down_b_ref[...]),
    ):
        own = own_ref[rows].astype(jnp.float32)
        summed = own + up.astype(jnp.float32) + down.astype(jnp.float32)
        gradient = summed.astype(jnp.bfloat16)
        gradient_ref[rows] = gradient
        grad_float = gradient.astype(jnp.float32)
        moment_new = (
            moment_decay * moment_ref[rows] + (1.0 - moment_decay) * grad_float * grad_float
        )
        moment_out_ref[rows] = moment_new
        adam_step = grad_float / (jnp.sqrt(moment_new) + adam_offset)
        total += jnp.sum(adam_step * adam_step)
    target_ref[...] = jnp.broadcast_to(jnp.sqrt(total), target_ref.shape)


def adam(sums, moment):
    return pl.pallas_call(
        adam_kernel,
        in_specs=[pl.BlockSpec(memory_space=pltpu.VMEM)] * 6,
        out_specs=[pl.BlockSpec(memory_space=pltpu.VMEM)] * 3,
        out_shape=[
            jax.ShapeDtypeStruct((B, B), jnp.bfloat16),
            jax.ShapeDtypeStruct((B, B), jnp.float32),
            jax.ShapeDtypeStruct((1, LANES), jnp.float32),
        ],
        compiler_params=pltpu.CompilerParams(vmem_limit_bytes=16 * 1024 * 1024),
        cost_estimate=pl.CostEstimate(flops=20*10**8, bytes_accessed=5 * 1024 * 1024, transcendentals=0),
        name="adam",
    )(*sums, moment)


def direction_kernel(in_ref, gradient_ref, target_ref, direction_ref, left_ref, right_ref):
    row, col = iotas((LANES, LANES))
    chunk = LANES // ROWS
    for i in range(QUARTERS):
        rows = slice(i * LANES, (i + 1) * LANES)
        members = slice(i * chunk, (i + 1) * chunk)
        tile = in_ref[members, QUARTERS].reshape(LANES, LANES).astype(jnp.float32)
        diagonal = jnp.sum(tile, axis=1, keepdims=True)
        for j in range(i, QUARTERS):
            cols = slice(j * LANES, (j + 1) * LANES)
            upper = in_ref[members, j].reshape(LANES, LANES).astype(jnp.float32)
            if i == j:
                turned = upper.T
                left_ref[rows, cols] = jnp.where(row <= col, upper, turned).astype(jnp.bfloat16)
                right = jnp.where(row > col, upper, turned)
                right_ref[rows, cols] = jnp.where(row == col, diagonal, right).astype(jnp.bfloat16)
            else:
                others = slice(j * chunk, (j + 1) * chunk)
                lower = in_ref[others, i].reshape(LANES, LANES).astype(jnp.float32)
                left_ref[rows, cols] = upper.astype(jnp.bfloat16)
                left_ref[cols, rows] = upper.T.astype(jnp.bfloat16)
                right_ref[cols, rows] = lower.astype(jnp.bfloat16)
                right_ref[rows, cols] = lower.T.astype(jnp.bfloat16)
    left_part = jnp.dot(left_ref[...], gradient_ref[...], preferred_element_type=jnp.float32)
    conditioned = jnp.dot(
        left_part.astype(jnp.bfloat16), right_ref[...], preferred_element_type=jnp.float32
    )
    scale = target_ref[:, :1] / jnp.sqrt(jnp.sum(conditioned * conditioned) + norm_offset)
    direction_ref[...] = (conditioned * scale).astype(jnp.bfloat16)


def direct(pieces, gradient, target):
    return pl.pallas_call(
        direction_kernel,
        in_specs=[pl.BlockSpec(memory_space=pltpu.VMEM)] * 3,
        out_specs=pl.BlockSpec(memory_space=pltpu.VMEM),
        out_shape=jax.ShapeDtypeStruct((B, B), jnp.bfloat16),
        scratch_shapes=[pltpu.VMEM((B, B), jnp.bfloat16)] * 2,
        compiler_params=pltpu.CompilerParams(vmem_limit_bytes=16 * 1024 * 1024),
        cost_estimate=pl.CostEstimate(
            flops=4 * B * B * B, bytes_accessed=2 * 1024 * 1024, transcendentals=0
        ),
        name="direction",
    )(pieces, gradient, target)


HALF = B // 2


def add_kernel(up_ref, down_ref, up_own_ref, down_own_ref, up_out_ref, down_out_ref):
    for in_ref, own_ref, out_ref in (
        (up_ref, up_own_ref, up_out_ref),
        (down_ref, down_own_ref, down_out_ref),
    ):
        total = in_ref[...].astype(jnp.float32) + own_ref[...].astype(jnp.float32)
        out_ref[...] = total.astype(jnp.bfloat16)


def add_own(up, down, own, name, flops=40*10**8):
    return pl.pallas_call(
        add_kernel,
        in_specs=[pl.BlockSpec(memory_space=pltpu.VMEM)] * (2 + len(own)),
        out_specs=[pl.BlockSpec(memory_space=pltpu.VMEM)] * 2,
        out_shape=[jax.ShapeDtypeStruct((HALF, B), jnp.bfloat16)] * 2,
        compiler_params=pltpu.CompilerParams(vmem_limit_bytes=8 * 1024 * 1024),
        cost_estimate=pl.CostEstimate(flops=flops, bytes_accessed=3 * 1024 * 1024, transcendentals=0),
        name=name,
    )(up, down, *own)


def reduce_chunks(partials, packed):
    groups = lax.axis_size("rep")
    pairs_up = [(k, (k + 1) % groups) for k in range(groups)]
    pairs_down = [(k, (k - 1) % groups) for k in range(groups)]

    def move(up, down):
        return lax.ppermute(up, "rep", pairs_up), lax.ppermute(down, "rep", pairs_down)

    def mine(offset, start=0, rows=B, source=partials):
        chunk = lax.rem(lax.axis_index("rep") + offset + groups, groups)
        return lax.dynamic_slice(source, (chunk * B + start, 0), (rows, B))

    def add(a, b):
        return (a.astype(jnp.float32) + b.astype(jnp.float32)).astype(jnp.bfloat16)

    def half(offset, part, source=partials):
        return mine(offset, part * HALF, HALF, source)

    def parts(step, part, source=partials):
        return [half(step, part, source), half(-step, 1 - part, source)]

    barrier = lax.optimization_barrier
    up, down = move(
        jnp.concatenate([half(4, 0), half(3, 1)]), jnp.concatenate([half(-3, 0), half(-4, 1)])
    )
    up, down, packed = barrier((up, down, packed))
    own = parts(3, 0)
    sent = barrier((add(up[:HALF], own[0]), add(down[HALF:], own[1])))
    long = move(*sent)
    up, down, later, _ = barrier((up, down, partials, sent))
    own = parts(2, 1, later)
    sent = barrier((add(up[HALF:], own[0]), add(down[:HALF], own[1])))
    short = move(*sent)
    later, _ = barrier((later, sent))
    long = move(*add_own(*long, parts(2, 0, later), "long_3"))
    sent = add_own(*short, parts(1, 1, later), "short_3")
    short = move(*sent)
    later, _ = barrier((later, sent))
    own = parts(1, 0, later)
    long = move(*barrier((add(long[0], own[0]), add(long[1], own[1]))))
    return mine(0, source=later), long[0], short[0], short[1], long[1]


def body(partials, moment, owner, roots):
    devices = lax.axis_size("shard")
    packed = pack(roots, devices)
    sums = reduce_chunks(partials[0], packed)
    pieces = lax.all_to_all(packed, "shard", split_axis=0, concat_axis=0, tiled=True)
    picked = pick(owner, pieces)
    arrived = lax.all_to_all(picked, "shard", split_axis=0, concat_axis=0, tiled=True)
    gradient, moment_new, target = adam(sums, moment)
    return direct(arrived, gradient, target), moment_new


def solution(mesh):
    placed = (
        P("rep", None, "shard"),
        P("rep", "shard"),
        P("rep", None),
        P("rep", "shard", None, None, None, None),
    )
    return jax.shard_map(
        body,
        mesh=mesh,
        in_specs=placed,
        out_specs=(P("rep", "shard"), P("rep", "shard")),
        check_vma=False,
    )
```

```python
import jax
import jax.numpy as jnp
from jax import lax
from jax.experimental import pallas as pl
from jax.experimental.pallas import tpu as pltpu
from jax.sharding import PartitionSpec as P

moment_decay = 0.95
adam_offset = 1e-08
norm_offset = 1e-06

B = 512
ROWS = 16
FULL = 60 * 1024 * 1024
LANES = 128
QUARTERS = B // LANES


def iotas(shape):
    return lax.broadcasted_iota(jnp.int32, shape, 0), lax.broadcasted_iota(jnp.int32, shape, 1)


def pack_kernel(roots_ref, result_ref, held, out_ref, sems, out_sems):
    slots = roots_ref.shape[2]
    tiles = result_ref.shape[1]
    chunk = LANES // ROWS
    copies = {}
    for k in range(slots):
        for i in range(QUARTERS):
            rows = slice(i * LANES, (i + 1) * LANES)
            for side, cols in ((0, slice(i * LANES, B)), (1, slice(0, (i + 1) * LANES))):
                copies[k, i, side] = pltpu.make_async_copy(
                    roots_ref.at[0, 0, k, side, rows, cols],
                    held.at[k, side, rows, cols],
                    sems.at[k, i, side],
                )
                copies[k, i, side].start()
    row, col = iotas((LANES, LANES))
    diagonal = [jnp.zeros((LANES, LANES), jnp.float32)] * QUARTERS
    stores = []
    for k in range(slots):
        for i in range(QUARTERS):
            rows = slice(i * LANES, (i + 1) * LANES)
            copies[k, i, 0].wait()
            copies[k, i, 1].wait()
            for j in range(QUARTERS):
                cols = slice(j * LANES, (j + 1) * LANES)
                if i == j:
                    right = held[k, 1, rows, cols]
                    block = jnp.where(row <= col, held[k, 0, rows, cols], right)
                    only = jnp.sum(jnp.where(row == col, right, 0.0), axis=1, keepdims=True)
                    diagonal[i] = jnp.where(col // 32 == k, only, diagonal[i])
                else:
                    block = held[k, 0 if i < j else 1, rows, cols]
                out_ref[i * chunk : (i + 1) * chunk, QUARTERS * k + j] = block.astype(
                    jnp.bfloat16
                ).reshape(chunk, ROWS, LANES)
            members = slice(i * chunk, (i + 1) * chunk)
            ready = slice(QUARTERS * k, QUARTERS * (k + 1))
            if k == slots - 1:
                out_ref[members, tiles - 1] = (
                    diagonal[i].astype(jnp.bfloat16).reshape(chunk, ROWS, LANES)
                )
                ready = slice(QUARTERS * k, tiles)
            stores.append(
                pltpu.make_async_copy(
                    out_ref.at[members, ready], result_ref.at[members, ready], out_sems.at[k, i]
                )
            )
            stores[-1].start()
    for store in stores:
        store.wait()


def pack(roots, devices):
    slots = roots.shape[2]
    tiles = QUARTERS * slots + 1
    return pl.pallas_call(
        pack_kernel,
        in_specs=[pl.BlockSpec(memory_space=pl.ANY)],
        out_specs=pl.BlockSpec(memory_space=pl.ANY),
        out_shape=jax.ShapeDtypeStruct((devices, tiles, ROWS, LANES), jnp.bfloat16),
        scratch_shapes=[
            pltpu.VMEM((slots, 2, B, B), jnp.float32),
            pltpu.VMEM((devices, tiles, ROWS, LANES), jnp.bfloat16),
            pltpu.SemaphoreType.DMA((slots, QUARTERS, 2)),
            pltpu.SemaphoreType.DMA((slots, QUARTERS)),
        ],
        compiler_params=pltpu.CompilerParams(vmem_limit_bytes=58 * 1024 * 1024),
        cost_estimate=pl.CostEstimate(flops=0, bytes_accessed=8 * 1024 * 1024, transcendentals=0),
        name="pack",
    )(roots)


def pick_kernel(owner_ref, in_ref, out_ref, counts):
    devices, tiles = in_ref.shape[:2]
    lane = lax.broadcasted_iota(jnp.int32, (ROWS, LANES), 1)
    for o in range(devices):
        counts[o] = 0
    owners = owner_ref[...]
    for c in range(out_ref.shape[0]):
        o = owners[0, c]
        slot = counts[o]
        counts[o] = slot + 1
        for q in range(QUARTERS):
            out_ref[c, q] = in_ref[o, QUARTERS * slot + q]
        diagonal = in_ref[o, tiles - 1].astype(jnp.float32)
        kept = jnp.where(lane == slot * 32, diagonal, 0.0)
        out_ref[c, QUARTERS] = kept.astype(jnp.bfloat16)


def pick(owner, pieces):
    cols = owner.shape[1]
    return pl.pallas_call(
        pick_kernel,
        in_specs=[pl.BlockSpec(memory_space=pltpu.VMEM)] * 2,
        out_specs=pl.BlockSpec(memory_space=pltpu.VMEM),
        out_shape=jax.ShapeDtypeStruct((cols, QUARTERS + 1, ROWS, LANES), jnp.bfloat16),
        scratch_shapes=[pltpu.SMEM((pieces.shape[0],), jnp.int32)],
        compiler_params=pltpu.CompilerParams(vmem_limit_bytes=8 * 1024 * 1024),
        cost_estimate=pl.CostEstimate(flops=0, bytes_accessed=3 * 1024 * 1024, transcendentals=0),
        name="pick",
    )(owner, pieces)


def ready_kernel(own_ref, up_b_ref, down_a_ref, known_ref):
    first, second = slice(0, HALF), slice(HALF, B)
    known_ref[first] = own_ref[first].astype(jnp.float32) + down_a_ref[...].astype(jnp.float32)
    known_ref[second] = own_ref[second].astype(jnp.float32) + up_b_ref[...].astype(jnp.float32)


def ready(own, up_b, down_a):
    return pl.pallas_call(
        ready_kernel,
        in_specs=[pl.BlockSpec(memory_space=pltpu.VMEM)] * 3,
        out_specs=pl.BlockSpec(memory_space=pltpu.VMEM),
        out_shape=jax.ShapeDtypeStruct((B, B), jnp.float32),
        compiler_params=pltpu.CompilerParams(vmem_limit_bytes=8 * 1024 * 1024),
        cost_estimate=pl.CostEstimate(flops=0, bytes_accessed=4 * 1024 * 1024, transcendentals=0),
        name="ready",
    )(own, up_b, down_a)


def adam_kernel(
    known_ref, moment_ref, up_a_ref, down_b_ref, gradient_ref, moment_out_ref, target_ref
):
    total = jnp.float32(0.0)
    for rows, last_ref in ((slice(0, HALF), up_a_ref), (slice(HALF, B), down_b_ref)):
        gradient = (known_ref[rows] + last_ref[...].astype(jnp.float32)).astype(jnp.bfloat16)
        gradient_ref[rows] = gradient
        grad_float = gradient.astype(jnp.float32)
        moment_new = moment_decay * moment_ref[rows] + (1.0 - moment_decay) * grad_float * grad_float
        moment_out_ref[rows] = moment_new
        adam_step = grad_float / (jnp.sqrt(moment_new) + adam_offset)
        total += jnp.sum(adam_step * adam_step)
    target_ref[...] = jnp.broadcast_to(jnp.sqrt(total), target_ref.shape)


def adam(known, moment, up_a, down_b):
    return pl.pallas_call(
        adam_kernel,
        in_specs=[pl.BlockSpec(memory_space=pltpu.VMEM)] * 4,
        out_specs=[pl.BlockSpec(memory_space=pltpu.VMEM)] * 3,
        out_shape=[
            jax.ShapeDtypeStruct((B, B), jnp.bfloat16),
            jax.ShapeDtypeStruct((B, B), jnp.float32),
            jax.ShapeDtypeStruct((1, LANES), jnp.float32),
        ],
        compiler_params=pltpu.CompilerParams(vmem_limit_bytes=8 * 1024 * 1024),
        cost_estimate=pl.CostEstimate(
            flops=20 * 10**8, bytes_accessed=5 * 1024 * 1024, transcendentals=0
        ),
        name="adam",
    )(known, moment, up_a, down_b)


def direction_kernel(in_ref, gradient_ref, target_ref, direction_ref, left_ref, right_ref):
    row, col = iotas((LANES, LANES))
    chunk = LANES // ROWS
    for i in range(QUARTERS):
        rows = slice(i * LANES, (i + 1) * LANES)
        members = slice(i * chunk, (i + 1) * chunk)
        tile = in_ref[members, QUARTERS].reshape(LANES, LANES).astype(jnp.float32)
        diagonal = jnp.sum(tile, axis=1, keepdims=True)
        for j in range(i, QUARTERS):
            cols = slice(j * LANES, (j + 1) * LANES)
            upper = in_ref[members, j].reshape(LANES, LANES).astype(jnp.float32)
            if i == j:
                turned = upper.T
                left_ref[rows, cols] = jnp.where(row <= col, upper, turned).astype(jnp.bfloat16)
                right = jnp.where(row > col, upper, turned)
                right_ref[rows, cols] = jnp.where(row == col, diagonal, right).astype(jnp.bfloat16)
            else:
                others = slice(j * chunk, (j + 1) * chunk)
                lower = in_ref[others, i].reshape(LANES, LANES).astype(jnp.float32)
                left_ref[rows, cols] = upper.astype(jnp.bfloat16)
                left_ref[cols, rows] = upper.T.astype(jnp.bfloat16)
                right_ref[cols, rows] = lower.astype(jnp.bfloat16)
                right_ref[rows, cols] = lower.T.astype(jnp.bfloat16)
    left_part = jnp.dot(left_ref[...], gradient_ref[...], preferred_element_type=jnp.float32)
    conditioned = jnp.dot(
        left_part.astype(jnp.bfloat16), right_ref[...], preferred_element_type=jnp.float32
    )
    scale = target_ref[:, :1] / jnp.sqrt(jnp.sum(conditioned * conditioned) + norm_offset)
    direction_ref[...] = (conditioned * scale).astype(jnp.bfloat16)


def direct(pieces, gradient, target):
    return pl.pallas_call(
        direction_kernel,
        in_specs=[pl.BlockSpec(memory_space=pltpu.VMEM)] * 3,
        out_specs=pl.BlockSpec(memory_space=pltpu.VMEM),
        out_shape=jax.ShapeDtypeStruct((B, B), jnp.bfloat16),
        scratch_shapes=[pltpu.VMEM((B, B), jnp.bfloat16)] * 2,
        compiler_params=pltpu.CompilerParams(vmem_limit_bytes=16 * 1024 * 1024),
        cost_estimate=pl.CostEstimate(
            flops=4 * B * B * B, bytes_accessed=2 * 1024 * 1024, transcendentals=0
        ),
        name="direction",
    )(pieces, gradient, target)


HALF = B // 2


def add_kernel(up_ref, down_ref, up_own_ref, down_own_ref, up_out_ref, down_out_ref):
    for in_ref, own_ref, out_ref in (
        (up_ref, up_own_ref, up_out_ref),
        (down_ref, down_own_ref, down_out_ref),
    ):
        total = in_ref[...].astype(jnp.float32) + own_ref[...].astype(jnp.float32)
        out_ref[...] = total.astype(jnp.bfloat16)


def add_own(up, down, own, name, flops=40*10**8):
    return pl.pallas_call(
        add_kernel,
        in_specs=[pl.BlockSpec(memory_space=pltpu.VMEM)] * (2 + len(own)),
        out_specs=[pl.BlockSpec(memory_space=pltpu.VMEM)] * 2,
        out_shape=[jax.ShapeDtypeStruct((HALF, B), jnp.bfloat16)] * 2,
        compiler_params=pltpu.CompilerParams(vmem_limit_bytes=8 * 1024 * 1024),
        cost_estimate=pl.CostEstimate(flops=flops, bytes_accessed=3 * 1024 * 1024, transcendentals=0),
        input_output_aliases={2: 0, 3: 1} if name == "short_3" else {},
        name=name,
    )(up, down, *own)


def reduce_chunks(partials, packed):
    groups = lax.axis_size("rep")
    pairs_up = [(k, (k + 1) % groups) for k in range(groups)]
    pairs_down = [(k, (k - 1) % groups) for k in range(groups)]

    def move(up, down):
        return lax.ppermute(up, "rep", pairs_up), lax.ppermute(down, "rep", pairs_down)

    def mine(offset, start=0, rows=B, source=partials):
        chunk = lax.rem(lax.axis_index("rep") + offset + groups, groups)
        return lax.dynamic_slice(source, (chunk * B + start, 0), (rows, B))

    def add(a, b):
        return (a.astype(jnp.float32) + b.astype(jnp.float32)).astype(jnp.bfloat16)

    def half(offset, part, source=partials):
        return mine(offset, part * HALF, HALF, source)

    def parts(step, part, source=partials):
        return [half(step, part, source), half(-step, 1 - part, source)]

    barrier = lax.optimization_barrier
    up, down = move(
        jnp.concatenate([half(4, 0), half(3, 1)]), jnp.concatenate([half(-3, 0), half(-4, 1)])
    )
    up, down, packed = barrier((up, down, packed))
    own = parts(3, 0)
    sent = barrier((add(up[:HALF], own[0]), add(down[HALF:], own[1])))
    long = move(*sent)
    up, down, later, _ = barrier((up, down, partials, sent))
    own = parts(2, 1, later)
    sent = barrier((add(up[HALF:], own[0]), add(down[:HALF], own[1])))
    short = move(*sent)
    later, _ = barrier((later, sent))
    long = move(*add_own(*long, parts(2, 0, later), "long_3"))
    sent = add_own(*short, parts(1, 1, later), "short_3")
    short = move(*sent)
    later, _ = barrier((later, sent))
    own = parts(1, 0, later)
    long = move(*barrier((add(long[0], own[0]), add(long[1], own[1]))))
    return mine(0, source=later), long[0], short[0], short[1], long[1]


def body(partials, moment, owner, roots):
    devices = lax.axis_size("shard")
    packed = pack(roots, devices)
    sums = reduce_chunks(partials[0], packed)
    pieces = lax.all_to_all(packed, "shard", split_axis=0, concat_axis=0, tiled=True)
    picked = pick(owner, pieces)
    arrived = lax.all_to_all(picked, "shard", split_axis=0, concat_axis=0, tiled=True)
    own, up_a, up_b, down_a, down_b = sums
    known = ready(own, up_b, down_a)
    gradient, moment_new, target = adam(known, moment, up_a, down_b)
    return direct(arrived, gradient, target), moment_new


def solution(mesh):
    placed = (
        P("rep", None, "shard"),
        P("rep", "shard"),
        P("rep", None),
        P("rep", "shard", None, None, None, None),
    )
    return jax.shard_map(
        body,
        mesh=mesh,
        in_specs=placed,
        out_specs=(P("rep", "shard"), P("rep", "shard")),
        check_vma=False,
    )
```

```python
import jax
import jax.numpy as jnp
from jax import lax
from jax.experimental import pallas as pl
from jax.experimental.pallas import tpu as pltpu
from jax.sharding import PartitionSpec as P

moment_decay = 0.95
adam_offset = 1e-08
norm_offset = 1e-06

B = 512
ROWS = 16
FULL = 60 * 1024 * 1024
LANES = 128
QUARTERS = B // LANES


def iotas(shape):
    return lax.broadcasted_iota(jnp.int32, shape, 0), lax.broadcasted_iota(jnp.int32, shape, 1)


def pack_kernel(roots_ref, result_ref, held, out_ref, sems, out_sems):
    slots = roots_ref.shape[2]
    tiles = result_ref.shape[1]
    chunk = LANES // ROWS
    copies = {}
    for k in range(slots):
        for i in range(QUARTERS):
            rows = slice(i * LANES, (i + 1) * LANES)
            for side, cols in ((0, slice(i * LANES, B)), (1, slice(0, (i + 1) * LANES))):
                copies[k, i, side] = pltpu.make_async_copy(
                    roots_ref.at[0, 0, k, side, rows, cols],
                    held.at[k, side, rows, cols],
                    sems.at[k, i, side],
                )
                copies[k, i, side].start()
    row, col = iotas((LANES, LANES))
    diagonal = [jnp.zeros((LANES, LANES), jnp.float32)] * QUARTERS
    stores = []
    for k in range(slots):
        for i in range(QUARTERS):
            rows = slice(i * LANES, (i + 1) * LANES)
            copies[k, i, 0].wait()
            copies[k, i, 1].wait()
            for j in range(QUARTERS):
                cols = slice(j * LANES, (j + 1) * LANES)
                if i == j:
                    right = held[k, 1, rows, cols]
                    block = jnp.where(row <= col, held[k, 0, rows, cols], right)
                    only = jnp.sum(jnp.where(row == col, right, 0.0), axis=1, keepdims=True)
                    diagonal[i] = jnp.where(col // 32 == k, only, diagonal[i])
                else:
                    block = held[k, 0 if i < j else 1, rows, cols]
                out_ref[i * chunk : (i + 1) * chunk, QUARTERS * k + j] = block.astype(
                    jnp.bfloat16
                ).reshape(chunk, ROWS, LANES)
            members = slice(i * chunk, (i + 1) * chunk)
            ready = slice(QUARTERS * k, QUARTERS * (k + 1))
            if k == slots - 1:
                out_ref[members, tiles - 1] = (
                    diagonal[i].astype(jnp.bfloat16).reshape(chunk, ROWS, LANES)
                )
                ready = slice(QUARTERS * k, tiles)
            stores.append(
                pltpu.make_async_copy(
                    out_ref.at[members, ready], result_ref.at[members, ready], out_sems.at[k, i]
                )
            )
            stores[-1].start()
    for store in stores:
        store.wait()


def pack(roots, devices):
    slots = roots.shape[2]
    tiles = QUARTERS * slots + 1
    return pl.pallas_call(
        pack_kernel,
        in_specs=[pl.BlockSpec(memory_space=pl.ANY)],
        out_specs=pl.BlockSpec(memory_space=pl.ANY),
        out_shape=jax.ShapeDtypeStruct((devices, tiles, ROWS, LANES), jnp.bfloat16),
        scratch_shapes=[
            pltpu.VMEM((slots, 2, B, B), jnp.float32),
            pltpu.VMEM((devices, tiles, ROWS, LANES), jnp.bfloat16),
            pltpu.SemaphoreType.DMA((slots, QUARTERS, 2)),
            pltpu.SemaphoreType.DMA((slots, QUARTERS)),
        ],
        compiler_params=pltpu.CompilerParams(vmem_limit_bytes=58 * 1024 * 1024),
        cost_estimate=pl.CostEstimate(flops=0, bytes_accessed=8 * 1024 * 1024, transcendentals=0),
        name="pack",
    )(roots)


def pick_kernel(owner_ref, in_ref, out_ref, counts):
    devices, tiles = in_ref.shape[:2]
    lane = lax.broadcasted_iota(jnp.int32, (ROWS, LANES), 1)
    for o in range(devices):
        counts[o] = 0
    owners = owner_ref[...]
    for c in range(out_ref.shape[0]):
        o = owners[0, c]
        slot = counts[o]
        counts[o] = slot + 1
        for q in range(QUARTERS):
            out_ref[c, q] = in_ref[o, QUARTERS * slot + q]
        diagonal = in_ref[o, tiles - 1].astype(jnp.float32)
        kept = jnp.where(lane == slot * 32, diagonal, 0.0)
        out_ref[c, QUARTERS] = kept.astype(jnp.bfloat16)


def pick(owner, pieces):
    cols = owner.shape[1]
    return pl.pallas_call(
        pick_kernel,
        in_specs=[pl.BlockSpec(memory_space=pltpu.VMEM)] * 2,
        out_specs=pl.BlockSpec(memory_space=pltpu.VMEM),
        out_shape=jax.ShapeDtypeStruct((cols, QUARTERS + 1, ROWS, LANES), jnp.bfloat16),
        scratch_shapes=[pltpu.SMEM((pieces.shape[0],), jnp.int32)],
        compiler_params=pltpu.CompilerParams(vmem_limit_bytes=8 * 1024 * 1024),
        cost_estimate=pl.CostEstimate(flops=0, bytes_accessed=3 * 1024 * 1024, transcendentals=0),
        name="pick",
    )(owner, pieces)


def ready_kernel(own_ref, up_b_ref, down_a_ref, known_ref):
    first, second = slice(0, HALF), slice(HALF, B)
    known_ref[first] = own_ref[first].astype(jnp.float32) + down_a_ref[...].astype(jnp.float32)
    known_ref[second] = own_ref[second].astype(jnp.float32) + up_b_ref[...].astype(jnp.float32)


def ready(own, up_b, down_a):
    return pl.pallas_call(
        ready_kernel,
        in_specs=[pl.BlockSpec(memory_space=pltpu.VMEM)] * 3,
        out_specs=pl.BlockSpec(memory_space=pltpu.VMEM),
        out_shape=jax.ShapeDtypeStruct((B, B), jnp.float32),
        compiler_params=pltpu.CompilerParams(vmem_limit_bytes=8 * 1024 * 1024),
        cost_estimate=pl.CostEstimate(flops=0, bytes_accessed=4 * 1024 * 1024, transcendentals=0),
        name="ready",
    )(own, up_b, down_a)


def adam_kernel(
    known_ref, moment_ref, up_a_ref, down_b_ref, gradient_ref, moment_out_ref, target_ref
):
    total = jnp.float32(0.0)
    for rows, last_ref in ((slice(0, HALF), up_a_ref), (slice(HALF, B), down_b_ref)):
        gradient = (known_ref[rows] + last_ref[...].astype(jnp.float32)).astype(jnp.bfloat16)
        gradient_ref[rows] = gradient
        grad_float = gradient.astype(jnp.float32)
        moment_new = moment_decay * moment_ref[rows] + (1.0 - moment_decay) * grad_float * grad_float
        moment_out_ref[rows] = moment_new
        adam_step = grad_float / (jnp.sqrt(moment_new) + adam_offset)
        total += jnp.sum(adam_step * adam_step)
    target_ref[...] = jnp.broadcast_to(jnp.sqrt(total), target_ref.shape)


def adam(known, moment, up_a, down_b):
    return pl.pallas_call(
        adam_kernel,
        in_specs=[pl.BlockSpec(memory_space=pltpu.VMEM)] * 4,
        out_specs=[pl.BlockSpec(memory_space=pltpu.VMEM)] * 3,
        out_shape=[
            jax.ShapeDtypeStruct((B, B), jnp.bfloat16),
            jax.ShapeDtypeStruct((B, B), jnp.float32),
            jax.ShapeDtypeStruct((1, LANES), jnp.float32),
        ],
        compiler_params=pltpu.CompilerParams(vmem_limit_bytes=8 * 1024 * 1024),
        cost_estimate=pl.CostEstimate(
            flops=20 * 10**8, bytes_accessed=5 * 1024 * 1024, transcendentals=0
        ),
        name="adam",
    )(known, moment, up_a, down_b)


def direction_kernel(in_ref, gradient_ref, target_ref, direction_ref, left_ref, right_ref):
    row, col = iotas((LANES, LANES))
    chunk = LANES // ROWS
    for i in range(QUARTERS):
        rows = slice(i * LANES, (i + 1) * LANES)
        members = slice(i * chunk, (i + 1) * chunk)
        tile = in_ref[members, QUARTERS].reshape(LANES, LANES).astype(jnp.float32)
        diagonal = jnp.sum(tile, axis=1, keepdims=True)
        for j in range(i, QUARTERS):
            cols = slice(j * LANES, (j + 1) * LANES)
            upper = in_ref[members, j].reshape(LANES, LANES).astype(jnp.float32)
            if i == j:
                turned = upper.T
                left_ref[rows, cols] = jnp.where(row <= col, upper, turned).astype(jnp.bfloat16)
                right = jnp.where(row > col, upper, turned)
                right_ref[rows, cols] = jnp.where(row == col, diagonal, right).astype(jnp.bfloat16)
            else:
                others = slice(j * chunk, (j + 1) * chunk)
                lower = in_ref[others, i].reshape(LANES, LANES).astype(jnp.float32)
                left_ref[rows, cols] = upper.astype(jnp.bfloat16)
                left_ref[cols, rows] = upper.T.astype(jnp.bfloat16)
                right_ref[cols, rows] = lower.astype(jnp.bfloat16)
                right_ref[rows, cols] = lower.T.astype(jnp.bfloat16)
    left_part = jnp.dot(left_ref[...], gradient_ref[...], preferred_element_type=jnp.float32)
    conditioned = jnp.dot(
        left_part.astype(jnp.bfloat16), right_ref[...], preferred_element_type=jnp.float32
    )
    scale = target_ref[:, :1] / jnp.sqrt(jnp.sum(conditioned * conditioned) + norm_offset)
    direction_ref[...] = (conditioned * scale).astype(jnp.bfloat16)


def direct(pieces, gradient, target):
    return pl.pallas_call(
        direction_kernel,
        in_specs=[pl.BlockSpec(memory_space=pltpu.VMEM)] * 3,
        out_specs=pl.BlockSpec(memory_space=pltpu.VMEM),
        out_shape=jax.ShapeDtypeStruct((B, B), jnp.bfloat16),
        scratch_shapes=[pltpu.VMEM((B, B), jnp.bfloat16)] * 2,
        compiler_params=pltpu.CompilerParams(vmem_limit_bytes=16 * 1024 * 1024),
        cost_estimate=pl.CostEstimate(
            flops=4 * B * B * B, bytes_accessed=2 * 1024 * 1024, transcendentals=0
        ),
        name="direction",
    )(pieces, gradient, target)


HALF = B // 2


def add_kernel(up_ref, down_ref, up_own_ref, down_own_ref, up_out_ref, down_out_ref):
    for in_ref, own_ref, out_ref in (
        (up_ref, up_own_ref, up_out_ref),
        (down_ref, down_own_ref, down_out_ref),
    ):
        total = in_ref[...].astype(jnp.float32) + own_ref[...].astype(jnp.float32)
        out_ref[...] = total.astype(jnp.bfloat16)


def add_own(up, down, own, name, flops=40*10**8):
    return pl.pallas_call(
        add_kernel,
        in_specs=[pl.BlockSpec(memory_space=pltpu.VMEM)] * (2 + len(own)),
        out_specs=[pl.BlockSpec(memory_space=pltpu.VMEM)] * 2,
        out_shape=[jax.ShapeDtypeStruct((HALF, B), jnp.bfloat16)] * 2,
        compiler_params=pltpu.CompilerParams(vmem_limit_bytes=8 * 1024 * 1024),
        cost_estimate=pl.CostEstimate(flops=flops, bytes_accessed=3 * 1024 * 1024, transcendentals=0),
        input_output_aliases={2: 0, 3: 1} if name == "long_3" else {},
        name=name,
    )(up, down, *own)


def reduce_chunks(partials, packed):
    groups = lax.axis_size("rep")
    pairs_up = [(k, (k + 1) % groups) for k in range(groups)]
    pairs_down = [(k, (k - 1) % groups) for k in range(groups)]

    def move(up, down):
        return lax.ppermute(up, "rep", pairs_up), lax.ppermute(down, "rep", pairs_down)

    def mine(offset, start=0, rows=B, source=partials):
        chunk = lax.rem(lax.axis_index("rep") + offset + groups, groups)
        return lax.dynamic_slice(source, (chunk * B + start, 0), (rows, B))

    def add(a, b):
        return (a.astype(jnp.float32) + b.astype(jnp.float32)).astype(jnp.bfloat16)

    def half(offset, part, source=partials):
        return mine(offset, part * HALF, HALF, source)

    def parts(step, part, source=partials):
        return [half(step, part, source), half(-step, 1 - part, source)]

    barrier = lax.optimization_barrier
    up, down = move(
        jnp.concatenate([half(4, 0), half(3, 1)]), jnp.concatenate([half(-3, 0), half(-4, 1)])
    )
    up, down, packed = barrier((up, down, packed))
    own = parts(3, 0)
    sent = barrier((add(up[:HALF], own[0]), add(down[HALF:], own[1])))
    long = move(*sent)
    up, down, later, _ = barrier((up, down, partials, sent))
    own = parts(2, 1, later)
    sent = barrier((add(up[HALF:], own[0]), add(down[:HALF], own[1])))
    short = move(*sent)
    later, _ = barrier((later, sent))
    long = move(*add_own(*long, parts(2, 0, later), "long_3"))
    sent = add_own(*short, parts(1, 1, later), "short_3")
    short = move(*sent)
    later, _ = barrier((later, sent))
    own = parts(1, 0, later)
    long = move(*barrier((add(long[0], own[0]), add(long[1], own[1]))))
    return mine(0, source=later), long[0], short[0], short[1], long[1]


def body(partials, moment, owner, roots):
    devices = lax.axis_size("shard")
    packed = pack(roots, devices)
    sums = reduce_chunks(partials[0], packed)
    pieces = lax.all_to_all(packed, "shard", split_axis=0, concat_axis=0, tiled=True)
    picked = pick(owner, pieces)
    arrived = lax.all_to_all(picked, "shard", split_axis=0, concat_axis=0, tiled=True)
    own, up_a, up_b, down_a, down_b = sums
    known = ready(own, up_b, down_a)
    gradient, moment_new, target = adam(known, moment, up_a, down_b)
    return direct(arrived, gradient, target), moment_new


def solution(mesh):
    placed = (
        P("rep", None, "shard"),
        P("rep", "shard"),
        P("rep", None),
        P("rep", "shard", None, None, None, None),
    )
    return jax.shard_map(
        body,
        mesh=mesh,
        in_specs=placed,
        out_specs=(P("rep", "shard"), P("rep", "shard")),
        check_vma=False,
    )
```
